512 devices in a mesh: dp: 32 (over z, y_lo), tensor: 16 (over x, y_hi, core).
Axes of the slice: x: 4, y: 4 (y_hi: 2, y_lo: 2; y = y_hi * 2 + y_lo), z: 16, core: 2. Of those that a mesh axis runs over, the one named last changes fastest.
Arguments:
- q_states: bfloat16 [65536, 4096], P(('dp', 'tensor')), may hold values from -500 to 500
- k_states: bfloat16 [65536, 512], P(('dp', 'tensor')), may hold values from -650 to 650
- v_states: bfloat16 [65536, 512], P(('dp', 'tensor')), may hold values from -6 to 6
- q_gain: float32 [128], replicated, may hold values from 0.3 to 7
- k_gain: float32 [128], replicated, may hold values from 0.3 to 7
- out_grad: bfloat16 [65536, 4096], P(('dp', 'tensor')), may hold values from -6 to 6
- lengths: int32 [32, 4], P('dp'), may hold values from 1 to 1024, 2048 in all within a row
- advantage: int32 [65536], P(('dp', 'tensor')), may hold values from -64 to 64
Outputs:
- q_grad: bfloat16 [65536, 4096], P(('dp', 'tensor'))
- k_grad: bfloat16 [65536, 512], P(('dp', 'tensor'))
- v_grad: bfloat16 [65536, 512], P(('dp', 'tensor'))
- gain_grad: float32 [2, 128], replicated
The draws below stay inside these ranges and needn't reach their ends.
All inputs are finite; a program needn't handle non-finite values.
Results may differ from the reference program's by a relative error of at most 0.02.
The reference program's roundings to bfloat16 on the way count: a program that leaves them out, or rounds other values in their place, can miss the bound.
Values may be sent and summed in bfloat16 or wider, within the bound.
No kernel may reach another device: no remote copies, remote signals or barrier semaphores. Data moves between devices by JAX's collectives and lax.ppermute only.
A program may use at most 128 MiB of HBM per device.

```python
import math
import jax
import jax.numpy as jnp
import numpy as np
from jax import lax

HD = 128
GROUP = 8
QHEADS = 32
KVHEADS = 4
L = 2048
TOKENS = 65536
MAXLEN = 1024
NRESP = 4
BQ = 256
KW = 1280
N_DP = 32


def scaled_normal(key, row_count, col_count):
    key_base, key_rows, key_cols = jax.random.split(key, 3)
    base = jnp.clip(jax.random.normal(key_base, (row_count, col_count), jnp.float32), -5.0, 5.0)
    row_scale = jnp.exp(jax.random.uniform(key_rows, (row_count, 1), jnp.float32) * math.log(10.0))
    col_scale = jnp.exp(jax.random.uniform(key_cols, (1, col_count), jnp.float32) * math.log(10.0))
    return base * row_scale * col_scale


def shared_states(key):
    key_query, key_key = jax.random.split(key)
    queries = scaled_normal(key_query, TOKENS, QHEADS * HD)
    key_rows = scaled_normal(key_key, TOKENS, KVHEADS * HD)
    return (queries, key_rows)


def gain_values(key, lower, upper):
    return jnp.exp(jax.random.uniform(key, (HD,), jnp.float32, math.log(lower), math.log(upper)))


def draw_q_states(key, part):
    queries, key_rows = shared_states(key)
    return queries.astype(jnp.bfloat16)


def draw_k_states(key, part):
    queries, key_rows = shared_states(key)
    return key_rows.astype(jnp.bfloat16)


def draw_q_gain(key, part):
    key = jax.random.fold_in(key, 7)
    return gain_values(key, 0.3, 1.2)


def draw_k_gain(key, part):
    key = jax.random.fold_in(key, 9)
    return gain_values(key, 0.3, 1.2)


def touch_ends(array, own_key, smallest, top_value):
    longest = array.shape.index(max(array.shape))
    spots = []
    for shift in (0, 1):
        where = [jax.random.randint(jax.random.fold_in(own_key, axis), (), 0, length) for axis, length in enumerate(array.shape)]
        where[longest] = (where[longest] + shift) % array.shape[longest]
        spots.append(tuple(where))
    return array.at[spots[0]].set(smallest).at[spots[1]].set(top_value)


def level_of(key, extent, cuts, smallest, high):
    def one(dim, blocks):
        steps = jax.random.uniform(jax.random.fold_in(jax.random.fold_in(key, 6), dim), (blocks,), jnp.float32, smallest / len(cuts), high / len(cuts))
        return jnp.repeat(jnp.exp(steps), extent[dim] // blocks).reshape((-1,) + (1,) * (len(extent) - dim - 1))

    gain = one(*cuts[0])
    for cut in cuts[1:]:
        gain = gain * one(*cut)
    return gain


def length_profile(amount, total, bound, lean):
    loads = [(1 << 20) // math.isqrt(grade ** lean) + 1 for grade in range(2, amount + 1)]
    rest, given = total - bound - (amount - 1), [1] * (amount - 1)
    while rest > 0:
        candidates = [i for i in range(amount - 1) if given[i] < bound]
        whole, budget = sum([loads[i] for i in candidates]), rest
        for i in candidates:
            more = min(bound - given[i], max(1, budget * loads[i] // whole), rest)
            given[i] = given[i] + more
            rest = rest - more
    return np.array([bound] + given)


def uneven(rng, amount, total, limit, slope):
    if amount == 2:
        one = jax.random.randint(rng, (), max(1, total - limit), min(limit, total - 1) + 1)
        return jnp.stack([one, total - one])
    sizes = jnp.asarray(length_profile(amount, total, limit, slope), jnp.int32)
    couples = (amount - 1) // 2
    donor, taker = sizes[1:1 + 2 * couples:2], sizes[2:2 + 2 * couples:2]
    room = jnp.minimum(donor - 1, limit - taker)
    moved = jax.random.randint(jax.random.fold_in(rng, 1), (couples,), 0, 1 << 20) % (room + 1)
    sizes = sizes.at[1:1 + 2 * couples:2].set(donor - moved).at[2:2 + 2 * couples:2].set(taker + moved)
    return sizes[jax.random.permutation(jax.random.fold_in(rng, 2), amount)]


def normal_values(own_key, extent, scale, limit, cuts=(), kind=jnp.bfloat16):
    entries = jax.random.normal(own_key, extent, jnp.float32) * scale
    if len(cuts) > 0:
        entries = level_of(own_key, extent, cuts, -0.22, 0.18) * entries
    return jnp.clip(entries, min=-limit, max=limit).astype(kind)


def setup_inputs(seed: int = 0) -> dict:
    keys = jax.random.split(jax.random.key(seed), 9)
    return {
        "q_states": draw_q_states(jax.random.fold_in(keys[8], 71), 0),
        "k_states": draw_k_states(jax.random.fold_in(keys[8], 71), 0),
        "v_states": normal_values(keys[2], (TOKENS, KVHEADS * HD), 1.0, 6.0, ((0, 512),)),
        "q_gain": draw_q_gain(jax.random.fold_in(keys[8], 71), 0),
        "k_gain": draw_k_gain(jax.random.fold_in(keys[8], 71), 0),
        "out_grad": normal_values(keys[5], (TOKENS, QHEADS * HD), 1.0, 6.0, ((0, 512),)),
        "lengths": jax.vmap(lambda own: uneven(own, NRESP, L, MAXLEN, 2))(jax.random.split(keys[6], N_DP)).reshape((N_DP, NRESP)).astype(jnp.int32),
        "advantage": touch_ends(jax.random.randint(keys[7], (TOKENS,), -64, 65), jax.random.fold_in(keys[7], 1), -64, 64).astype(jnp.int32),
    }


rope_base = 1000000.0
norm_eps = 1e-06

def response_layout(lens, group_rows):
    end_marks = jnp.cumsum(lens).astype(jnp.int32)
    token_place = jnp.arange(group_rows, dtype=jnp.int32)
    has_ended = end_marks[None, :] <= token_place[:, None]
    resp_start = lax.optimization_barrier(jnp.sum(jnp.where(has_ended, lens[None, :], 0), axis=1)).astype(jnp.int32)
    segment = lax.optimization_barrier(jnp.sum(has_ended.astype(jnp.int32), axis=1)).astype(jnp.int32)
    owner_mask = segment[:, None] == jnp.arange(lens.shape[0], dtype=jnp.int32)[None, :]
    length = lax.optimization_barrier(jnp.sum(jnp.where(owner_mask, lens[None, :], 0), axis=1)).astype(jnp.int32)
    return (token_place - resp_start, segment, length)

def rope_tables(position, head_width):
    half_width = head_width // 2
    frequency = rope_base ** (-jnp.arange(half_width, dtype=jnp.float32) * 2.0 / head_width)
    angles = position.astype(jnp.float32)[:, None] * frequency[None, :]
    cosine = jnp.concatenate([jnp.cos(angles), jnp.cos(angles)], axis=1)
    sine_table = jnp.concatenate([jnp.sin(angles), jnp.sin(angles)], axis=1)
    return (cosine[:, None, :], sine_table[:, None, :])

def half_turn(values):
    half_width = values.shape[-1] // 2
    return jnp.concatenate([-values[..., half_width:], values[..., :half_width]], axis=-1)

def turn_back(values):
    half_width = values.shape[-1] // 2
    return jnp.concatenate([values[..., half_width:], -values[..., :half_width]], axis=-1)

def norm_rope(states, gain_vec, cosine, sine_table):
    values = states.astype(jnp.float32)
    rms_scale = jnp.sqrt(lax.optimization_barrier(jnp.mean(values * values, axis=-1, keepdims=True)) + norm_eps)
    unit_rows = values / rms_scale
    scaled = unit_rows * gain_vec
    turned = scaled * cosine + half_turn(scaled) * sine_table
    return (turned.astype(jnp.bfloat16), unit_rows, rms_scale)

def norm_rope_back(upstream, unit_rows, rms_scale, gain_vec, cosine, sine_table):
    d_scaled = upstream * cosine + turn_back(upstream * sine_table)
    gain_part = lax.optimization_barrier(jnp.sum(d_scaled * unit_rows, axis=(0, 1)))
    d_unit = d_scaled * gain_vec
    d_states = (d_unit - unit_rows * lax.optimization_barrier(jnp.mean(d_unit * unit_rows, axis=-1, keepdims=True))) / rms_scale
    return (d_states.astype(jnp.bfloat16), gain_part)

def group_grads(q_rows, k_rows, v_rows, grad_rows, lens, adv_rows, q_gain, k_gain):
    position, segment, length = response_layout(lens, L)
    cosine, sine_table = rope_tables(position, HD)
    q_turned, q_unit, q_scale = norm_rope(q_rows.reshape(L, QHEADS, HD), q_gain, cosine, sine_table)
    k_turned, k_unit, k_scale = norm_rope(k_rows.reshape(L, KVHEADS, HD), k_gain, cosine, sine_table)
    weight = adv_rows.astype(jnp.float32) / 32.0 * (L / NRESP) / length.astype(jnp.float32)
    d_out = (grad_rows.astype(jnp.float32).reshape(L, QHEADS, HD) * weight[:, None, None]).astype(jnp.bfloat16)
    query_rows = q_turned.reshape(L, KVHEADS, GROUP, HD).astype(jnp.float32)
    key_rows = k_turned.astype(jnp.float32)
    value_rows = v_rows.reshape(L, KVHEADS, HD).astype(jnp.float32)
    dout_rows = d_out.reshape(L, KVHEADS, GROUP, HD).astype(jnp.float32)
    score_scale = 1.0 / math.sqrt(HD)

    def attend(state_pair, step_index):
        d_keys, d_values = state_pair
        q_first = (step_index * BQ).astype(jnp.int32)
        k_first = jnp.clip(q_first - MAXLEN, 0, L - KW).astype(jnp.int32)
        q_block = lax.dynamic_slice_in_dim(query_rows, q_first, BQ, 0)
        g_block = lax.dynamic_slice_in_dim(dout_rows, q_first, BQ, 0)
        k_block = lax.dynamic_slice_in_dim(key_rows, k_first, KW, 0)
        v_block = lax.dynamic_slice_in_dim(value_rows, k_first, KW, 0)
        q_place = q_first + jnp.arange(BQ, dtype=jnp.int32)
        k_place = k_first + jnp.arange(KW, dtype=jnp.int32)
        q_seg = lax.dynamic_slice_in_dim(segment, q_first, BQ, 0)
        k_seg = lax.dynamic_slice_in_dim(segment, k_first, KW, 0)
        allowed = (k_place[None, :] <= q_place[:, None]) & (k_seg[None, :] == q_seg[:, None])
        scores = jnp.einsum('igrd,jgd->grij', q_block, k_block) * score_scale
        scores = jnp.where(allowed, scores, -1e+30)
        peak = lax.optimization_barrier(jnp.max(scores, axis=-1, keepdims=True))
        expo_rows = jnp.exp(scores - peak)
        prob_block = expo_rows / lax.optimization_barrier(jnp.sum(expo_rows, axis=-1, keepdims=True))
        prob_round = lax.optimization_barrier(prob_block.astype(jnp.bfloat16)).astype(jnp.float32)
        dv_part = jnp.einsum('grij,igrd->jgd', prob_round, g_block)
        d_prob = jnp.einsum('igrd,jgd->grij', g_block, v_block)
        row_delta = lax.optimization_barrier(jnp.sum(prob_block * d_prob, axis=-1, keepdims=True))
        d_score = prob_block * (d_prob - row_delta) * score_scale
        d_score = lax.optimization_barrier(d_score.astype(jnp.bfloat16)).astype(jnp.float32)
        dq_block = jnp.einsum('grij,jgd->igrd', d_score, k_block)
        dk_part = jnp.einsum('grij,igrd->jgd', d_score, q_block)
        d_keys = lax.dynamic_update_slice_in_dim(d_keys, lax.dynamic_slice_in_dim(d_keys, k_first, KW, 0) + dk_part, k_first, 0)
        d_values = lax.dynamic_update_slice_in_dim(d_values, lax.dynamic_slice_in_dim(d_values, k_first, KW, 0) + dv_part, k_first, 0)
        return ((d_keys, d_values), dq_block)
    empty_rows = jnp.zeros((L, KVHEADS, HD), jnp.float32)
    (d_keys, d_values), dq_blocks = lax.scan(attend, (empty_rows, empty_rows), jnp.arange(L // BQ, dtype=jnp.int32))
    d_queries = dq_blocks.reshape(L, QHEADS, HD)
    q_grad, q_part = norm_rope_back(d_queries, q_unit, q_scale, q_gain, cosine, sine_table)
    k_grad, k_part = norm_rope_back(d_keys, k_unit, k_scale, k_gain, cosine, sine_table)
    return (q_grad.reshape(L, QHEADS * HD), k_grad.reshape(L, KVHEADS * HD), d_values.astype(jnp.bfloat16).reshape(L, KVHEADS * HD), jnp.stack([q_part, k_part]))

def reference(q_states, k_states, v_states, q_gain, k_gain, out_grad, lengths, advantage):

    def one_group(pieces):
        return group_grads(pieces[0], pieces[1], pieces[2], pieces[3], pieces[4], pieces[5], q_gain, k_gain)
    q_grad, k_grad, v_grad, parts = lax.map(one_group, (q_states.reshape(N_DP, L, QHEADS * HD), k_states.reshape(N_DP, L, KVHEADS * HD), v_states.reshape(N_DP, L, KVHEADS * HD), out_grad.reshape(N_DP, L, QHEADS * HD), lengths, advantage.reshape(N_DP, L)))
    gain_grad = lax.optimization_barrier(jnp.sum(parts, axis=0)) / L
    return (q_grad.reshape(TOKENS, QHEADS * HD), k_grad.reshape(TOKENS, KVHEADS * HD), v_grad.reshape(TOKENS, KVHEADS * HD), gain_grad)
```

```python
import math

import jax
import jax.numpy as jnp
from jax import lax
from jax.experimental import pallas as pl
from jax.experimental.pallas import tpu as pltpu
from jax.sharding import PartitionSpec as P

HD = 128
GROUP = 8
ROWS = 128
CHIP = 2 * ROWS
BACK = 4
WIN = (BACK + 1) * CHIP
SPAN = BACK * CHIP + ROWS
PAIR = 2 * ROWS
STRIP = 16

rope_base = 1000000.0
norm_eps = 1e-06
far = -1e30
SCALE = 1.0 / math.sqrt(HD)
SCALE2 = SCALE * math.log2(math.e)
f32 = jnp.float32
bf16 = jnp.bfloat16


def unit_of(raw):
    x = raw.astype(f32)
    inv = lax.rsqrt(jnp.mean(x * x, axis=-1, keepdims=True) + norm_eps)
    return x * inv, inv


def turn(scaled, cos, sin):
    return scaled * cos + pltpu.roll(scaled, HD // 2, 1) * sin


def norm_back(d, unit, inv, gain, cos, sin):
    d_scaled = d * cos - pltpu.roll(d, HD // 2, 1) * sin
    prod = d_scaled * unit
    d_unit = d_scaled * gain
    mean = jnp.mean(prod * gain, axis=-1, keepdims=True)
    part = jnp.sum(prod.reshape(prod.shape[0] // 8, 8, HD), axis=0)
    return (d_unit - unit * mean) * inv, part


def attend_kernel(
    core_ref, q_own, g_own, rq, kv4, kv3, kv2, kv1, kv0, cos, sin, kaug, qaug, wt, qgain, kgain,
    dq_own, dq_far, dkv4, dkv3, dkv2, dkv1, dkv0, gains,
    kt, vt, qt, gt, s_a, s_b, dp_a, dp_b, p_scr, ds_scr, dk_acc, dv_acc,
):
    core = core_ref[0]
    blocks = (kv4, kv3, kv2, kv1, kv0)
    kg = kgain[...]
    qg = qgain[...]
    for i, blk in enumerate(blocks):
        rows = slice(i * CHIP, (i + 1) * CHIP)
        unit, _ = unit_of(blk[:, :HD])
        kt[rows, :HD] = turn(unit * kg, cos[rows, :], sin[rows, :]).astype(bf16)
        kt[rows, HD:] = kaug[rows, :]
        vt[rows, :] = blk[:, HD:]
    offs = []
    for j in range(2):
        b = core if j == 0 else 1 - core
        off = pl.multiple_of(b * ROWS, ROWS)
        offs.append(off)
        c = cos[pl.ds(BACK * CHIP + off, ROWS), :]
        s = sin[pl.ds(BACK * CHIP + off, ROWS), :]
        hot = qaug[pl.ds(off, ROWS), :]
        for h in range(GROUP):
            cols = slice(h * HD, (h + 1) * HD)
            rows = slice(h * ROWS, (h + 1) * ROWS)
            raw = q_own[:, cols] if j == 0 else rq[:, cols]
            unit, _ = unit_of(raw)
            qt[j, rows, :HD] = turn(unit * qg, c, s).astype(bf16)
            qt[j, rows, HD:] = hot
            if j == 0:
                gt[j, rows, :] = (g_own[:, cols].astype(f32) * wt[...]).astype(bf16)
            else:
                gt[j, rows, :] = rq[:, GROUP * HD + h * HD : GROUP * HD + (h + 1) * HD]

    dk_acc[...] = jnp.zeros_like(dk_acc)
    dv_acc[...] = jnp.zeros_like(dv_acc)
    s_buf = (s_a, s_b)
    dp_buf = (dp_a, dp_b)
    tiles = [(j, hp) for j in range(2) for hp in range(GROUP // 2)]
    causal = [
        lax.broadcasted_iota(jnp.int32, (STRIP, ROWS), 1)
        <= lax.broadcasted_iota(jnp.int32, (STRIP, ROWS), 0) + o
        for o in range(0, ROWS, STRIP)
    ]
    nt = (((1,), (1,)), ((), ()))
    tn = (((0,), (0,)), ((), ()))
    gain_rows = [jnp.zeros((8, HD), f32)]

    def scores(n):
        j, hp = tiles[n]
        rows = slice(hp * PAIR, (hp + 1) * PAIR)
        kw = kt[pl.ds(offs[j], SPAN), :]
        vw = vt[pl.ds(offs[j], SPAN), :]
        s_buf[n % 2][...] = lax.dot_general(qt[j, rows, :], kw, nt, preferred_element_type=f32)
        dp_buf[n % 2][...] = lax.dot_general(gt[j, rows, :], vw, nt, preferred_element_type=f32)

    def soft(n):
        j, hp = tiles[n]
        for r in range(0, PAIR, STRIP):
            s = s_buf[n % 2][r : r + STRIP, :]
            dp = dp_buf[n % 2][r : r + STRIP, :]
            tail = jnp.where(causal[(r % ROWS) // STRIP], s[:, SPAN - ROWS :], far)
            s = jnp.concatenate([s[:, : SPAN - ROWS], tail], axis=1)
            m = jnp.max(s, axis=-1, keepdims=True)
            e = jnp.exp2((s - m) * SCALE2)
            inv = 1.0 / jnp.sum(e, axis=-1, keepdims=True)
            delta = jnp.sum(e * dp, axis=-1, keepdims=True) * inv
            out = slice(hp * PAIR + r, hp * PAIR + r + STRIP)
            p_scr[j, out, :] = (e * inv).astype(bf16)
            ds_scr[j, out, :] = (e * (dp - delta) * (inv * SCALE)).astype(bf16)

    def grads(n):
        j, hp = tiles[n]
        rows = slice(hp * PAIR, (hp + 1) * PAIR)
        kw = kt[pl.ds(offs[j], SPAN), :HD]
        dq = lax.dot_general(ds_scr[j, rows, :], kw, (((1,), (0,)), ((), ())), preferred_element_type=f32)
        c = cos[pl.ds(BACK * CHIP + offs[j], ROWS), :]
        s = sin[pl.ds(BACK * CHIP + offs[j], ROWS), :]
        for u in range(2):
            h = hp * 2 + u
            cols = slice(h * HD, (h + 1) * HD)
            raw = q_own[:, cols] if j == 0 else rq[:, cols]
            unit, inv = unit_of(raw)
            grad, part = norm_back(dq[u * ROWS : (u + 1) * ROWS, :], unit, inv, qg, c, s)
            gain_rows[0] = gain_rows[0] + part
            if j == 0:
                dq_own[:, cols] = grad.astype(bf16)
            else:
                dq_far[:, cols] = grad.astype(bf16)
        if hp % 2 == 1:
            both = slice((hp - 1) * PAIR, (hp + 1) * PAIR)
            keys = pl.ds(offs[j], SPAN)
            dv_acc[keys, :] += lax.dot_general(p_scr[j, both, :], gt[j, both, :], tn, preferred_element_type=f32)
            dk_acc[keys, :] += lax.dot_general(ds_scr[j, both, :], qt[j, both, :HD], tn, preferred_element_type=f32)

    total = len(tiles)
    for n in range(total + 2):
        if n < total:
            scores(n)
        if 0 <= n - 1 < total:
            soft(n - 1)
        if 0 <= n - 2 < total:
            grads(n - 2)

    k_rows = jnp.zeros((8, HD), f32)
    for i, (blk, out) in enumerate(zip(blocks, (dkv4, dkv3, dkv2, dkv1, dkv0))):
        rows = slice(i * CHIP, (i + 1) * CHIP)
        unit, inv = unit_of(blk[:, :HD])
        grad, part = norm_back(dk_acc[rows, :], unit, inv, kg, cos[rows, :], sin[rows, :])
        k_rows = k_rows + part
        out[:, :HD] = grad.astype(out.dtype)
        out[:, HD:] = dv_acc[rows, :].astype(out.dtype)
    gains[:8, :] = gain_rows[0]
    gains[8:, :] = k_rows


def attend(head, core, q_states, out_grad, rq, kvs, cos, sin, kaug, qaug, wt, qgain, kgain):
    wide = GROUP * HD

    def whole(shape):
        return pl.BlockSpec(shape, lambda i, c: (0,) * len(shape))

    mine = pl.BlockSpec((ROWS, wide), lambda i, c: (0, 2 * c[0] + head))
    sds = jax.ShapeDtypeStruct
    back = sds((CHIP, 2 * HD), bf16)
    pairs = 2 * 2 * GROUP * ROWS * SPAN
    return pl.pallas_call(
        attend_kernel,
        grid_spec=pltpu.PrefetchScalarGridSpec(
            num_scalar_prefetch=1,
            grid=(1,),
            in_specs=[mine, mine, whole((ROWS, 2 * wide))]
            + [whole((CHIP, 2 * HD))] * (BACK + 1)
            + [whole((WIN, HD))] * 3
            + [whole((CHIP, HD)), whole((ROWS, 1)), whole((1, HD)), whole((1, HD))],
            out_specs=[whole((ROWS, wide))] * 2 + [whole((CHIP, 2 * HD))] * (BACK + 1) + [whole((16, HD))],
            scratch_shapes=[
                pltpu.VMEM((WIN, 2 * HD), bf16),
                pltpu.VMEM((WIN, HD), bf16),
                pltpu.VMEM((2, GROUP * ROWS, 2 * HD), bf16),
                pltpu.VMEM((2, GROUP * ROWS, HD), bf16),
                pltpu.VMEM((PAIR, SPAN), f32),
                pltpu.VMEM((PAIR, SPAN), f32),
                pltpu.VMEM((PAIR, SPAN), f32),
                pltpu.VMEM((PAIR, SPAN), f32),
                pltpu.VMEM((2, GROUP * ROWS, SPAN), bf16),
                pltpu.VMEM((2, GROUP * ROWS, SPAN), bf16),
                pltpu.VMEM((WIN, HD), f32),
                pltpu.VMEM((WIN, HD), f32),
            ],
        ),
        out_shape=[sds((ROWS, wide), bf16)] * 2 + [back] * BACK + [sds((CHIP, 2 * HD), f32), sds((16, HD), f32)],
        compiler_params=pltpu.CompilerParams(vmem_limit_bytes=40 * 2**20),
        cost_estimate=pl.CostEstimate(flops=pairs * HD * 2 * 5, bytes_accessed=4 * 2**20, transcendentals=pairs),
        name="attend_back",
    )(core, q_states, out_grad, rq, *kvs, cos, sin, kaug, qaug, wt, qgain, kgain)


def window_layout(lens, first):
    ends = jnp.cumsum(lens)
    token = first - BACK * CHIP + jnp.arange(WIN, dtype=jnp.int32)
    ended = ends[None, :] <= token[:, None]
    start = jnp.sum(jnp.where(ended, lens[None, :], 0), axis=1)
    segment = jnp.sum(ended.astype(jnp.int32), axis=1)
    owner = segment[:, None] == jnp.arange(lens.shape[0], dtype=jnp.int32)[None, :]
    length = jnp.sum(jnp.where(owner, lens[None, :], 0), axis=1)
    return jnp.where(token < 0, -1, segment), token - start, length


def local(q_states, k_states, v_states, q_gain, k_gain, out_grad, lengths, advantage):
    size = lax.axis_size("tensor")
    pos = lax.axis_index("tensor")
    core = pos % 2
    chip = pos // 2
    chips = size // 2
    group_rows = size * ROWS
    wide = GROUP * HD

    segment, position, length = window_layout(lengths[0], chip * CHIP)
    frequency = rope_base ** (-jnp.arange(HD // 2, dtype=f32) * 2.0 / HD)
    angles = position.astype(f32)[:, None] * frequency[None, :]
    c, s = jnp.cos(angles), jnp.sin(angles)
    cos = jnp.concatenate([c, c], axis=1)
    sin = jnp.concatenate([-s, s], axis=1)
    lane = jnp.arange(HD, dtype=jnp.int32)[None, :]
    same = segment[:, None] == lane
    kaug = jnp.where(same | (lane >= lengths.shape[1]), 0.0, far).astype(bf16)
    qaug = same[BACK * CHIP :].astype(bf16)
    own_len = lax.dynamic_slice_in_dim(length, BACK * CHIP + core * ROWS, ROWS, 0)
    weight = advantage.astype(f32) / 32.0 * (group_rows / lengths.shape[1]) / own_len.astype(f32)
    wt = weight[:, None]

    swap = [(t, t ^ 1) for t in range(size)]

    def heads_of(x, g, width):
        return lax.dynamic_slice_in_dim(x, g * width, width, 1)

    def half(who):
        return jnp.concatenate(
            [heads_of(y, 2 * who + g, HD) for g in range(2) for y in (k_states, v_states)], axis=1
        )

    kv_mine = half(core)
    kv_other = lax.ppermute(half(1 - core), "tensor", swap)
    first, second = (jnp.where(core == 0, a, b) for a, b in ((kv_mine, kv_other), (kv_other, kv_mine)))
    kv_chip = jnp.concatenate([first, second], axis=0)

    rqs, kvs = [], []
    for g in range(2):
        kv = kv_chip[:, g * 2 * HD : (g + 1) * 2 * HD]
        kvs.append(
            [
                lax.ppermute(kv, "tensor", [(t, t + 2 * n) for t in range(size - 2 * n)])
                for n in range(BACK, 0, -1)
            ]
            + [kv]
        )
        head = 2 * (1 - core) + g
        d_far = (heads_of(out_grad, head, wide).astype(f32) * wt).astype(bf16)
        rqs.append(
            lax.ppermute(jnp.concatenate([heads_of(q_states, head, wide), d_far], axis=1), "tensor", swap)
        )

    core_arr = core.astype(jnp.int32)[None]
    dq_mine, dq_back, dkv_sum, gain_rows = [], [], [], 0.0
    for g in range(2):
        outs = attend(
            g, core_arr, q_states, out_grad, rqs[g], kvs[g], cos, sin, kaug, qaug, wt, q_gain[None], k_gain[None]
        )
        dq_mine.append(outs[0])
        dq_back.append(lax.ppermute(outs[1], "tensor", swap))
        total = outs[2 + BACK]
        for n, part in zip(range(BACK, 0, -1), outs[2 : 2 + BACK]):
            part = lax.ppermute(part, "tensor", [(t + 2 * n, t) for t in range(size - 2 * n)])
            total = total + part.astype(f32)
        dkv_sum.append(total)
        gain_rows = gain_rows + outs[3 + BACK]

    gains = jnp.sum(gain_rows.reshape(2, 8, HD), axis=1)
    gains = jnp.pad(gains, ((0, 6), (0, 0)))
    for axis in ("tensor", "dp"):
        n = lax.axis_size(axis)
        spread = jnp.broadcast_to(gains[None], (n, 8, HD))
        gains = jnp.sum(lax.all_to_all(spread, axis, 0, 0, tiled=True), axis=0)
    gain_grad = gains[:2] / group_rows

    dkv = jnp.concatenate(dkv_sum, axis=1).astype(bf16)
    dkv_mine = lax.dynamic_slice_in_dim(dkv, core * ROWS, ROWS, 0)
    dkv_far = lax.ppermute(lax.dynamic_slice_in_dim(dkv, (1 - core) * ROWS, ROWS, 0), "tensor", swap)

    def placed(mine, other):
        return jnp.where(
            core == 0, jnp.concatenate([mine, other], axis=1), jnp.concatenate([other, mine], axis=1)
        )

    def part_of(x, which):
        return jnp.concatenate([x[:, which * HD : (which + 1) * HD], x[:, (2 + which) * HD : (3 + which) * HD]], axis=1)

    k_grad = placed(part_of(dkv_mine, 0), part_of(dkv_far, 0))
    v_grad = placed(part_of(dkv_mine, 1), part_of(dkv_far, 1))
    q_grad = placed(jnp.concatenate(dq_mine, axis=1), jnp.concatenate(dq_back, axis=1))
    return q_grad, k_grad, v_grad, gain_grad


def solution(mesh):
    return jax.shard_map(
        local,
        mesh=mesh,
        in_specs=(
            P(("dp", "tensor"), None),
            P(("dp", "tensor"), None),
            P(("dp", "tensor"), None),
            P(),
            P(),
            P(("dp", "tensor"), None),
            P("dp", None),
            P(("dp", "tensor")),
        ),
        out_specs=(
            P(("dp", "tensor"), None),
            P(("dp", "tensor"), None),
            P(("dp", "tensor"), None),
            P(),
        ),
        check_vma=False,
    )
```

```python
import math

import jax
import jax.numpy as jnp
from jax import lax
from jax.experimental import pallas as pl
from jax.experimental.pallas import tpu as pltpu
from jax.sharding import PartitionSpec as P

HD = 128
GROUP = 8
ROWS = 128
CHIP = 2 * ROWS
HEADS = 2
BACK = 4
WIN = (BACK + 1) * CHIP
SPAN = BACK * CHIP + ROWS
PART = SPAN // 3
SUB = 64
PAIR = 2 * ROWS

rope_base = 1000000.0
norm_eps = 1e-06
far = -1e30
SCALE = 1.0 / math.sqrt(HD)
SCALE2 = SCALE * math.log2(math.e)
f32 = jnp.float32
bf16 = jnp.bfloat16


def unit_of(raw):
    x = raw.astype(f32)
    inv = lax.rsqrt(jnp.mean(x * x, axis=-1, keepdims=True) + norm_eps)
    return x * inv, inv


def turn(scaled, cos, sin):
    return scaled * cos + pltpu.roll(scaled, HD // 2, 1) * sin


def norm_back(d, unit, inv, gain, cos, sin):
    d_scaled = d * cos - pltpu.roll(d, HD // 2, 1) * sin
    prod = d_scaled * unit
    d_unit = d_scaled * gain
    mean = jnp.mean(prod * gain, axis=-1, keepdims=True)
    part = jnp.sum(prod.reshape(prod.shape[0] // 8, 8, HD), axis=0)
    return (d_unit - unit * mean) * inv, part


def attend_kernel(
    core_ref, q_own, g_own, rq, kv_far, kv2, kv1, kv0, cos, sin, kaug, qaug, wt, qgain, kgain,
    dq_own, dq_far, dkv4, dkv3, dkv2, dkv1, dkv0, gains,
    kt, vt, qt, gt, s_buf, dp_buf, p_scr, ds_scr, dk_acc, dv_acc,
):
    core = core_ref[0]
    blocks = (kv_far.at[:CHIP], kv_far.at[CHIP:], kv2, kv1, kv0)
    d_blocks = (dkv4, dkv3, dkv2, dkv1, dkv0)
    kg = kgain[...]
    qg = qgain[...]
    for i, blk in enumerate(blocks):
        rows = slice(i * CHIP, (i + 1) * CHIP)
        unit, _ = unit_of(blk[:, :HD])
        kt[rows, :HD] = turn(unit * kg, cos[rows, :], sin[rows, :]).astype(bf16)
        kt[rows, HD:] = kaug[rows, :]
        vt[rows, :] = blk[:, HD:]
    offs = []
    for j in range(2):
        b = core if j == 0 else 1 - core
        off = pl.multiple_of(b * ROWS, ROWS)
        offs.append(off)
        c = cos[pl.ds(BACK * CHIP + off, ROWS), :]
        s = sin[pl.ds(BACK * CHIP + off, ROWS), :]
        hot = qaug[pl.ds(off, ROWS), :]
        for h in range(GROUP):
            cols = slice(h * HD, (h + 1) * HD)
            rows = slice(h * ROWS, (h + 1) * ROWS)
            raw = q_own[:, cols] if j == 0 else rq[:, cols]
            unit, _ = unit_of(raw)
            qt[j, rows, :HD] = turn(unit * qg, c, s).astype(bf16)
            qt[j, rows, HD:] = hot
            if j == 0:
                gt[j, rows, :] = (g_own[:, cols].astype(f32) * wt[...]).astype(bf16)
            else:
                gt[j, rows, :] = rq[:, GROUP * HD + h * HD : GROUP * HD + (h + 1) * HD]

    dk_acc[...] = jnp.zeros_like(dk_acc)
    dv_acc[...] = jnp.zeros_like(dv_acc)
    tiles = [(j, hp) for j in range(2) for hp in range(GROUP // 2)]
    total = len(tiles)
    chunks = SPAN // PART
    nt = (((1,), (1,)), ((), ()))
    tn = (((0,), (0,)), ((), ()))
    nn = (((1,), (0,)), ((), ()))
    key_row = lax.broadcasted_iota(jnp.int32, (ROWS, PAIR), 0)
    query = lax.broadcasted_iota(jnp.int32, (ROWS, PAIR), 1) % ROWS
    causal = key_row <= query
    gain_rows = [jnp.zeros((8, HD), f32)]
    peaks, sums, dots, shift, delta = {}, {}, {}, {}, {}

    def fold(x, op):
        out = x[:8]
        for r in range(8, x.shape[0], 8):
            out = op(out, x[r : r + 8])
        return out

    def cols_of(n):
        hp = tiles[n][1]
        return slice(hp * PAIR, (hp + 1) * PAIR)

    def keys_of(n, c):
        return pl.ds(pl.multiple_of(offs[tiles[n][0]] + c * PART, ROWS), PART)

    def scores(n, c):
        j = tiles[n][0]
        here = slice(c * PART, (c + 1) * PART)
        s = lax.dot_general(kt[keys_of(n, c), :], qt[j, cols_of(n), :], nt, preferred_element_type=f32)
        if c == chunks - 1:
            s = jnp.concatenate([s[: PART - ROWS], jnp.where(causal, s[PART - ROWS :], far)], axis=0)
        s_buf[n % 3, here, :] = s
        top = fold(s, jnp.maximum)
        peaks[n] = jnp.maximum(peaks[n], top) if c else top
        dp_buf[n % 3, here, :] = lax.dot_general(
            vt[keys_of(n, c), :], gt[j, cols_of(n), :], nt, preferred_element_type=f32
        )

    def weights(n, c):
        if c == 0:
            shift[n] = jnp.max(peaks[n], axis=0, keepdims=True) * SCALE2
            sums[n] = dots[n] = 0.0
        for r in range(c * PART, (c + 1) * PART, SUB):
            e = jnp.exp2(s_buf[n % 3, r : r + SUB, :] * SCALE2 - shift[n])
            sums[n] = sums[n] + fold(e, jnp.add)
            dots[n] = dots[n] + fold(e * dp_buf[n % 3, r : r + SUB, :], jnp.add)

    def slopes(n, c):
        if c == 0:
            norm = jnp.sum(sums[n], axis=0, keepdims=True)
            delta[n] = jnp.sum(dots[n], axis=0, keepdims=True) / norm
            shift[n] = shift[n] + jnp.log2(norm)
        j = tiles[n][0]
        for r in range(c * PART, (c + 1) * PART, SUB):
            p = jnp.exp2(s_buf[n % 3, r : r + SUB, :] * SCALE2 - shift[n])
            p_scr[j, r : r + SUB, cols_of(n)] = p.astype(bf16)
            ds_scr[j, r : r + SUB, cols_of(n)] = (p * (dp_buf[n % 3, r : r + SUB, :] - delta[n]) * SCALE).astype(bf16)

    def query_grads(n):
        j, hp = tiles[n]
        kw = kt[pl.ds(offs[j], SPAN), :HD]
        dq = lax.dot_general(ds_scr[j, :, cols_of(n)], kw, tn, preferred_element_type=f32)
        c = cos[pl.ds(BACK * CHIP + offs[j], ROWS), :]
        s = sin[pl.ds(BACK * CHIP + offs[j], ROWS), :]
        for u in range(2):
            h = hp * 2 + u
            cols = slice(h * HD, (h + 1) * HD)
            raw = q_own[:, cols] if j == 0 else rq[:, cols]
            unit, inv = unit_of(raw)
            grad, part = norm_back(dq[u * ROWS : (u + 1) * ROWS, :], unit, inv, qg, c, s)
            gain_rows[0] = gain_rows[0] + part
            if j == 0:
                dq_own[:, cols] = grad.astype(bf16)
            else:
                dq_far[:, cols] = grad.astype(bf16)

    def key_grads(n, c):
        j, hp = tiles[n]
        both = slice((hp - 1) * PAIR, (hp + 1) * PAIR)
        here = slice(c * PART, (c + 1) * PART)
        keys = keys_of(n, c)
        dv_acc[keys, :] += lax.dot_general(p_scr[j, here, both], gt[j, both, :], nn, preferred_element_type=f32)
        dk_acc[keys, :] += lax.dot_general(ds_scr[j, here, both], qt[j, both, :HD], nn, preferred_element_type=f32)

    for step in range(total + 3):
        for c in range(chunks):
            if step < total:
                scores(step, c)
            if 0 <= step - 1 < total:
                weights(step - 1, c)
            if 0 <= step - 2 < total:
                slopes(step - 2, c)
            n = step - 3
            if 0 <= n < total and n % 2 == 1:
                key_grads(n, c)
        if 0 <= step - 3 < total:
            query_grads(step - 3)

    k_rows = jnp.zeros((8, HD), f32)
    for i, (blk, out) in enumerate(zip(blocks, d_blocks)):
        rows = slice(i * CHIP, (i + 1) * CHIP)
        unit, inv = unit_of(blk[:, :HD])
        grad, part = norm_back(dk_acc[rows, :], unit, inv, kg, cos[rows, :], sin[rows, :])
        k_rows = k_rows + part
        out[:, :HD] = grad.astype(out.dtype)
        out[:, HD:] = dv_acc[rows, :].astype(out.dtype)
    rows = jnp.concatenate([gain_rows[0], k_rows], axis=0)
    begun = pl.program_id(0) > 0
    gains[...] = rows + jnp.where(begun, gains[...], 0.0)


def attend(core, q_states, out_grad, rq, kvs, cos, sin, kaug, qaug, wt, qgain, kgain):
    wide = GROUP * HD

    def whole(shape):
        return pl.BlockSpec(shape, lambda g, c: (0,) * len(shape))

    def column(shape):
        return pl.BlockSpec(shape, lambda g, c: (0, g))

    mine = pl.BlockSpec((ROWS, wide), lambda g, c: (0, 2 * c[0] + g))
    sds = jax.ShapeDtypeStruct
    pairs = HEADS * 2 * GROUP * ROWS * SPAN
    return pl.pallas_call(
        attend_kernel,
        grid_spec=pltpu.PrefetchScalarGridSpec(
            num_scalar_prefetch=1,
            grid=(HEADS,),
            in_specs=[mine, mine, column((ROWS, 2 * wide))]
            + [column((2 * CHIP, 2 * HD))] + [column((CHIP, 2 * HD))] * 3
            + [whole((WIN, HD))] * 3
            + [whole((CHIP, HD)), whole((ROWS, 1)), whole((1, HD)), whole((1, HD))],
            out_specs=[column((ROWS, wide))] * 2
            + [column((CHIP, 2 * HD))] * (BACK + 1)
            + [whole((16, HD))],
            scratch_shapes=[
                pltpu.VMEM((WIN, 2 * HD), bf16),
                pltpu.VMEM((WIN, HD), bf16),
                pltpu.VMEM((2, GROUP * ROWS, 2 * HD), bf16),
                pltpu.VMEM((2, GROUP * ROWS, HD), bf16),
                pltpu.VMEM((3, SPAN, PAIR), f32),
                pltpu.VMEM((3, SPAN, PAIR), f32),
                pltpu.VMEM((2, SPAN, GROUP * ROWS), bf16),
                pltpu.VMEM((2, SPAN, GROUP * ROWS), bf16),
                pltpu.VMEM((WIN, HD), f32),
                pltpu.VMEM((WIN, HD), f32),
            ],
        ),
        out_shape=[sds((ROWS, HEADS * wide), bf16)] * 2
        + [sds((CHIP, HEADS * 2 * HD), bf16)] * BACK
        + [sds((CHIP, HEADS * 2 * HD), f32), sds((16, HD), f32)],
        compiler_params=pltpu.CompilerParams(vmem_limit_bytes=58 * 2**20),
        cost_estimate=pl.CostEstimate(flops=pairs * HD * 2 * 5, bytes_accessed=4 * 2**20, transcendentals=pairs),
        name="attend_back",
    )(core, q_states, out_grad, rq, *kvs, cos, sin, kaug, qaug, wt, qgain, kgain)


def window_layout(lens, first):
    ends = jnp.cumsum(lens)
    token = first - BACK * CHIP + jnp.arange(WIN, dtype=jnp.int32)
    ended = ends[None, :] <= token[:, None]
    start = jnp.sum(jnp.where(ended, lens[None, :], 0), axis=1)
    segment = jnp.sum(ended.astype(jnp.int32), axis=1)
    owner = segment[:, None] == jnp.arange(lens.shape[0], dtype=jnp.int32)[None, :]
    length = jnp.sum(jnp.where(owner, lens[None, :], 0), axis=1)
    return jnp.where(token < 0, -1, segment), token - start, length


def local(q_states, k_states, v_states, q_gain, k_gain, out_grad, lengths, advantage):
    size = lax.axis_size("tensor")
    pos = lax.axis_index("tensor")
    core = pos % 2
    chip = pos // 2
    chips = size // 2
    group_rows = size * ROWS
    wide = GROUP * HD

    swap = [(t, t ^ 1) for t in range(size)]

    def heads_of(x, g, width):
        return lax.dynamic_slice_in_dim(x, g * width, width, 1)

    def half(who):
        return jnp.concatenate(
            [heads_of(y, HEADS * who + g, HD) for g in range(HEADS) for y in (k_states, v_states)], axis=1
        )

    kv_mine = half(core)
    kv_other = lax.ppermute(half(1 - core), "tensor", swap)
    first, second = (jnp.where(core == 0, a, b) for a, b in ((kv_mine, kv_other), (kv_other, kv_mine)))
    kv_chip = jnp.concatenate([first, second], axis=0)
    kv_chip, lens, q_states, out_grad = lax.optimization_barrier((kv_chip, lengths[0], q_states, out_grad))
    def later(x, n):
        return lax.ppermute(x, "tensor", [(t, t + 2 * n) for t in range(size - 2 * n)])

    kv1, kv2 = later(kv_chip, 1), later(kv_chip, 2)
    kvs = [later(jnp.concatenate([kv2, kv1], axis=0), 2), kv2, kv1, kv_chip]

    segment, position, length = window_layout(lens, chip * CHIP)
    frequency = rope_base ** (-jnp.arange(HD // 2, dtype=f32) * 2.0 / HD)
    angles = position.astype(f32)[:, None] * frequency[None, :]
    c, s = jnp.cos(angles), jnp.sin(angles)
    cos = jnp.concatenate([c, c], axis=1)
    sin = jnp.concatenate([-s, s], axis=1)
    lane = jnp.arange(HD, dtype=jnp.int32)[None, :]
    same = segment[:, None] == lane
    kaug = jnp.where(same | (lane >= lengths.shape[1]), 0.0, far).astype(bf16)
    qaug = same[BACK * CHIP :].astype(bf16)
    own_len = lax.dynamic_slice_in_dim(length, BACK * CHIP + core * ROWS, ROWS, 0)
    weight = advantage.astype(f32) / 32.0 * (group_rows / lengths.shape[1]) / own_len.astype(f32)
    wt = weight[:, None]

    pieces = []
    for g in range(HEADS):
        head = HEADS * (1 - core) + g
        pieces += [heads_of(q_states, head, wide), (heads_of(out_grad, head, wide).astype(f32) * wt).astype(bf16)]
    rq = lax.ppermute(jnp.concatenate(pieces, axis=1), "tensor", swap)

    outs = attend(
        core.astype(jnp.int32)[None], q_states, out_grad, rq, kvs, cos, sin, kaug, qaug, wt, q_gain[None], k_gain[None]
    )
    dq_mine, dq_far, *parts, dkv, gain_rows = outs

    gains = jnp.sum(gain_rows.reshape(2, 8, HD), axis=1)
    gains = gains.reshape(1, 2 * HD)

    def gathered_sum(x, axis):
        n = lax.axis_size(axis)
        spread = jnp.broadcast_to(x[None], (n, 1, 2 * HD))
        return jnp.sum(lax.all_to_all(spread, axis, 0, 0, tiled=True), axis=0)

    dq_back = lax.ppermute(dq_far, "tensor", swap)

    def earlier(x, n):
        return lax.ppermute(x, "tensor", [(t + 2 * n, t) for t in range(size - 2 * n)])

    back = [earlier(part, n) for n, part in zip(range(BACK, 0, -1), parts)]
    gains, back = lax.optimization_barrier((gathered_sum(gains, "dp"), back))
    gain_grad = gathered_sum(gains, "tensor").reshape(2, HD) / group_rows
    for part in back:
        dkv = dkv + part.astype(f32)
    dkv = dkv.astype(bf16)
    dkv_mine = lax.dynamic_slice_in_dim(dkv, core * ROWS, ROWS, 0)
    dkv_far = lax.ppermute(lax.dynamic_slice_in_dim(dkv, (1 - core) * ROWS, ROWS, 0), "tensor", swap)

    def placed(mine, other):
        return jnp.where(
            core == 0, jnp.concatenate([mine, other], axis=1), jnp.concatenate([other, mine], axis=1)
        )

    def part_of(x, which):
        return jnp.concatenate([x[:, (2 * g + which) * HD : (2 * g + which + 1) * HD] for g in range(HEADS)], axis=1)

    k_grad = placed(part_of(dkv_mine, 0), part_of(dkv_far, 0))
    v_grad = placed(part_of(dkv_mine, 1), part_of(dkv_far, 1))
    q_grad = placed(dq_mine, dq_back)
    return q_grad, k_grad, v_grad, gain_grad


def solution(mesh):
    return jax.shard_map(
        local,
        mesh=mesh,
        in_specs=(
            P(("dp", "tensor"), None),
            P(("dp", "tensor"), None),
            P(("dp", "tensor"), None),
            P(),
            P(),
            P(("dp", "tensor"), None),
            P("dp", None),
            P(("dp", "tensor")),
        ),
        out_specs=(
            P(("dp", "tensor"), None),
            P(("dp", "tensor"), None),
            P(("dp", "tensor"), None),
            P(),
        ),
        check_vma=False,
    )
```

```python
import math

import jax
import jax.numpy as jnp
from jax import lax
from jax.experimental import pallas as pl
from jax.experimental.pallas import tpu as pltpu
from jax.sharding import PartitionSpec as P

HD = 128
GROUP = 8
ROWS = 128
CHIP = 2 * ROWS
HEADS = 2
BACK = 4
WIN = (BACK + 1) * CHIP
SPAN = BACK * CHIP + ROWS
PART = SPAN // 3
SUB = 64
PAIR = 2 * ROWS

rope_base = 1000000.0
norm_eps = 1e-06
far = -1e30
SCALE = 1.0 / math.sqrt(HD)
SCALE2 = SCALE * math.log2(math.e)
f32 = jnp.float32
bf16 = jnp.bfloat16


def unit_of(raw):
    x = raw.astype(f32)
    inv = lax.rsqrt(jnp.mean(x * x, axis=-1, keepdims=True) + norm_eps)
    return x * inv, inv


def turn(scaled, cos, sin):
    return scaled * cos + pltpu.roll(scaled, HD // 2, 1) * sin


def norm_back(d, unit, inv, gain, cos, sin):
    d_scaled = d * cos - pltpu.roll(d, HD // 2, 1) * sin
    prod = d_scaled * unit
    d_unit = d_scaled * gain
    mean = jnp.mean(prod * gain, axis=-1, keepdims=True)
    part = jnp.sum(prod.reshape(prod.shape[0] // 8, 8, HD), axis=0)
    return (d_unit - unit * mean) * inv, part


def attend_kernel(
    core_ref, qt, gt, q_own, q_far, kv_far, kv2, kv1, kv0, cos, sin, kaug, qgain, kgain,
    dq_own, dq_far, dkv4, dkv3, dkv2, dkv1, dkv0, gains,
    kt, vt, s_buf, dp_buf, p_scr, ds_scr, dk_acc, dv_acc,
):
    core = core_ref[0]
    blocks = (kv_far.at[:CHIP], kv_far.at[CHIP:], kv2, kv1, kv0)
    d_blocks = (dkv4, dkv3, dkv2, dkv1, dkv0)
    kg = kgain[...]
    qg = qgain[...]
    for i, blk in enumerate(blocks):
        rows = slice(i * CHIP, (i + 1) * CHIP)
        unit, _ = unit_of(blk[:, :HD])
        kt[rows, :HD] = turn(unit * kg, cos[rows, :], sin[rows, :]).astype(bf16)
        kt[rows, HD:] = kaug[rows, :]
        vt[rows, :] = blk[:, HD:]
    offs = [pl.multiple_of(b * ROWS, ROWS) for b in (core, 1 - core)]

    dk_acc[...] = jnp.zeros_like(dk_acc)
    dv_acc[...] = jnp.zeros_like(dv_acc)
    tiles = [(j, hp) for j in range(2) for hp in range(GROUP // 2)]
    total = len(tiles)
    chunks = SPAN // PART
    nt = (((1,), (1,)), ((), ()))
    tn = (((0,), (0,)), ((), ()))
    nn = (((1,), (0,)), ((), ()))
    key_row = lax.broadcasted_iota(jnp.int32, (ROWS, PAIR), 0)
    query = lax.broadcasted_iota(jnp.int32, (ROWS, PAIR), 1) % ROWS
    causal = key_row <= query
    gain_rows = [jnp.zeros((8, HD), f32)]
    peaks, sums, dots, shift, delta = {}, {}, {}, {}, {}

    def fold(x, op):
        out = x[:8]
        for r in range(8, x.shape[0], 8):
            out = op(out, x[r : r + 8])
        return out

    def cols_of(n):
        hp = tiles[n][1]
        return slice(hp * PAIR, (hp + 1) * PAIR)

    def keys_of(n, c):
        return pl.ds(pl.multiple_of(offs[tiles[n][0]] + c * PART, ROWS), PART)

    def scores(n, c):
        j = tiles[n][0]
        here = slice(c * PART, (c + 1) * PART)
        s = lax.dot_general(kt[keys_of(n, c), :], qt[0, j, cols_of(n), :], nt, preferred_element_type=f32)
        if c == chunks - 1:
            s = jnp.concatenate([s[: PART - ROWS], jnp.where(causal, s[PART - ROWS :], far)], axis=0)
        s_buf[n % 3, here, :] = s
        top = fold(s, jnp.maximum)
        peaks[n] = jnp.maximum(peaks[n], top) if c else top
        dp_buf[n % 3, here, :] = lax.dot_general(
            vt[keys_of(n, c), :], gt[0, j, cols_of(n), :], nt, preferred_element_type=f32
        )

    def weights(n, c):
        if c == 0:
            shift[n] = jnp.max(peaks[n], axis=0, keepdims=True) * SCALE2
            sums[n] = dots[n] = 0.0
        for r in range(c * PART, (c + 1) * PART, SUB):
            e = jnp.exp2(s_buf[n % 3, r : r + SUB, :] * SCALE2 - shift[n])
            sums[n] = sums[n] + fold(e, jnp.add)
            dots[n] = dots[n] + fold(e * dp_buf[n % 3, r : r + SUB, :], jnp.add)

    def slopes(n, c):
        if c == 0:
            norm = jnp.sum(sums[n], axis=0, keepdims=True)
            delta[n] = jnp.sum(dots[n], axis=0, keepdims=True) / norm
            shift[n] = shift[n] + jnp.log2(norm)
        j = tiles[n][0]
        for r in range(c * PART, (c + 1) * PART, SUB):
            p = jnp.exp2(s_buf[n % 3, r : r + SUB, :] * SCALE2 - shift[n])
            p_scr[j, r : r + SUB, cols_of(n)] = p.astype(bf16)
            ds_scr[j, r : r + SUB, cols_of(n)] = (p * (dp_buf[n % 3, r : r + SUB, :] - delta[n]) * SCALE).astype(bf16)

    def query_grads(n):
        j, hp = tiles[n]
        kw = kt[pl.ds(offs[j], SPAN), :HD]
        dq = lax.dot_general(ds_scr[j, :, cols_of(n)], kw, tn, preferred_element_type=f32)
        c = cos[pl.ds(BACK * CHIP + offs[j], ROWS), :]
        s = sin[pl.ds(BACK * CHIP + offs[j], ROWS), :]
        for u in range(2):
            h = hp * 2 + u
            cols = slice(h * HD, (h + 1) * HD)
            raw = q_own[:, cols] if j == 0 else q_far[:, cols]
            unit, inv = unit_of(raw)
            grad, part = norm_back(dq[u * ROWS : (u + 1) * ROWS, :], unit, inv, qg, c, s)
            gain_rows[0] = gain_rows[0] + part
            if j == 0:
                dq_own[:, cols] = grad.astype(bf16)
            else:
                dq_far[:, cols] = grad.astype(bf16)

    def key_grads(n, c):
        j, hp = tiles[n]
        both = slice((hp - 1) * PAIR, (hp + 1) * PAIR)
        here = slice(c * PART, (c + 1) * PART)
        keys = keys_of(n, c)
        dv_acc[keys, :] += lax.dot_general(p_scr[j, here, both], gt[0, j, both, :], nn, preferred_element_type=f32)
        dk_acc[keys, :] += lax.dot_general(ds_scr[j, here, both], qt[0, j, both, :HD], nn, preferred_element_type=f32)

    for step in range(total + 3):
        for c in range(chunks):
            if step < total:
                scores(step, c)
            if 0 <= step - 1 < total:
                weights(step - 1, c)
            if 0 <= step - 2 < total:
                slopes(step - 2, c)
            n = step - 3
            if 0 <= n < total and n % 2 == 1:
                key_grads(n, c)
        if 0 <= step - 3 < total:
            query_grads(step - 3)

    k_rows = jnp.zeros((8, HD), f32)
    for i, (blk, out) in enumerate(zip(blocks, d_blocks)):
        rows = slice(i * CHIP, (i + 1) * CHIP)
        unit, inv = unit_of(blk[:, :HD])
        grad, part = norm_back(dk_acc[rows, :], unit, inv, kg, cos[rows, :], sin[rows, :])
        k_rows = k_rows + part
        out[:, :HD] = grad.astype(out.dtype)
        out[:, HD:] = dv_acc[rows, :].astype(out.dtype)
    rows = jnp.concatenate([gain_rows[0], k_rows], axis=0)
    begun = pl.program_id(0) > 0
    gains[...] = rows + jnp.where(begun, gains[...], 0.0)


def query_kernel(core_ref, q_own, g_own, rq, cos, sin, qaug, wt, qgain, qt, gt):
    core = core_ref[0]
    gain = qgain[...]
    for j in range(2):
        at = pl.ds(pl.multiple_of((core if j == 0 else 1 - core) * ROWS, ROWS), ROWS)
        c, s, hot = cos[at, :], sin[at, :], qaug[at, :]
        for h in range(GROUP):
            cols = slice(h * HD, (h + 1) * HD)
            rows = slice(h * ROWS, (h + 1) * ROWS)
            unit, _ = unit_of(q_own[:, cols] if j == 0 else rq[:, cols])
            qt[0, j, rows, :HD] = turn(unit * gain, c, s).astype(bf16)
            qt[0, j, rows, HD:] = hot
            grad = g_own[:, cols] if j == 0 else rq[:, GROUP * HD + h * HD : GROUP * HD + (h + 1) * HD]
            gt[0, j, rows, :] = (grad.astype(f32) * wt[:, j : j + 1]).astype(bf16)


def queries(core, q_states, out_grad, rq, cos, sin, qaug, wt, qgain):
    wide = GROUP * HD

    def whole(shape, at=(0, 0)):
        return pl.BlockSpec(shape, lambda g, c: at)

    mine = pl.BlockSpec((ROWS, wide), lambda g, c: (0, 2 * c[0] + g))
    own_rows = whole((CHIP, HD), (BACK, 0))
    out = (HEADS, 2, GROUP * ROWS)
    size = 1
    for n in out:
        size *= n
    return pl.pallas_call(
        query_kernel,
        grid_spec=pltpu.PrefetchScalarGridSpec(
            num_scalar_prefetch=1,
            grid=(HEADS,),
            in_specs=[mine, mine, pl.BlockSpec((ROWS, 2 * wide), lambda g, c: (0, g)), own_rows, own_rows]
            + [whole((CHIP, HD)), whole((ROWS, 2)), whole((1, HD))],
            out_specs=[
                pl.BlockSpec((1, 2, GROUP * ROWS, n), lambda g, c: (g, 0, 0, 0)) for n in (2 * HD, HD)
            ],
        ),
        out_shape=[jax.ShapeDtypeStruct(out + (n,), bf16) for n in (2 * HD, HD)],
        compiler_params=pltpu.CompilerParams(vmem_limit_bytes=38 * 2**20),
        cost_estimate=pl.CostEstimate(flops=40 * size * HD, bytes_accessed=5 * 2**20, transcendentals=size),
        name="queries",
    )(core, q_states, out_grad, rq, cos, sin, qaug, wt, qgain)


def attend(core, qt, gt, q_states, rq, kvs, cos, sin, kaug, qgain, kgain):
    wide = GROUP * HD

    def whole(shape):
        return pl.BlockSpec(shape, lambda g, c: (0,) * len(shape))

    def column(shape):
        return pl.BlockSpec(shape, lambda g, c: (0, g))

    mine = pl.BlockSpec((ROWS, wide), lambda g, c: (0, 2 * c[0] + g))
    sds = jax.ShapeDtypeStruct
    pairs = HEADS * 2 * GROUP * ROWS * SPAN
    return pl.pallas_call(
        attend_kernel,
        grid_spec=pltpu.PrefetchScalarGridSpec(
            num_scalar_prefetch=1,
            grid=(HEADS,),
            in_specs=[
                pl.BlockSpec((1, 2, GROUP * ROWS, n), lambda g, c: (g, 0, 0, 0)) for n in (2 * HD, HD)
            ]
            + [mine, pl.BlockSpec((ROWS, wide), lambda g, c: (0, 2 * g))]
            + [column((2 * CHIP, 2 * HD))] + [column((CHIP, 2 * HD))] * 3
            + [whole((WIN, HD))] * 3
            + [whole((1, HD)), whole((1, HD))],
            out_specs=[column((ROWS, wide))] * 2
            + [column((CHIP, 2 * HD))] * (BACK + 1)
            + [whole((16, HD))],
            scratch_shapes=[
                pltpu.VMEM((WIN, 2 * HD), bf16),
                pltpu.VMEM((WIN, HD), bf16),
                pltpu.VMEM((3, SPAN, PAIR), f32),
                pltpu.VMEM((3, SPAN, PAIR), f32),
                pltpu.VMEM((2, SPAN, GROUP * ROWS), bf16),
                pltpu.VMEM((2, SPAN, GROUP * ROWS), bf16),
                pltpu.VMEM((WIN, HD), f32),
                pltpu.VMEM((WIN, HD), f32),
            ],
        ),
        out_shape=[sds((ROWS, HEADS * wide), bf16)] * 2
        + [sds((CHIP, HEADS * 2 * HD), bf16)] * BACK
        + [sds((CHIP, HEADS * 2 * HD), f32), sds((16, HD), f32)],
        compiler_params=pltpu.CompilerParams(vmem_limit_bytes=38 * 2**20),
        cost_estimate=pl.CostEstimate(flops=pairs * HD * 2 * 5, bytes_accessed=4 * 2**20, transcendentals=pairs),
        name="attend_back",
    )(core, qt, gt, q_states, rq, *kvs, cos, sin, kaug, qgain, kgain)


def window_layout(lens, first):
    ends = jnp.cumsum(lens)
    token = first - BACK * CHIP + jnp.arange(WIN, dtype=jnp.int32)
    ended = ends[None, :] <= token[:, None]
    start = jnp.sum(jnp.where(ended, lens[None, :], 0), axis=1)
    segment = jnp.sum(ended.astype(jnp.int32), axis=1)
    owner = segment[:, None] == jnp.arange(lens.shape[0], dtype=jnp.int32)[None, :]
    length = jnp.sum(jnp.where(owner, lens[None, :], 0), axis=1)
    return jnp.where(token < 0, -1, segment), token - start, length


def local(q_states, k_states, v_states, q_gain, k_gain, out_grad, lengths, advantage):
    size = lax.axis_size("tensor")
    pos = lax.axis_index("tensor")
    core = pos % 2
    chip = pos // 2
    chips = size // 2
    group_rows = size * ROWS
    wide = GROUP * HD

    swap = [(t, t ^ 1) for t in range(size)]

    def heads_of(x, g, width):
        return lax.dynamic_slice_in_dim(x, g * width, width, 1)

    def half(who):
        return jnp.concatenate(
            [heads_of(y, HEADS * who + g, HD) for g in range(HEADS) for y in (k_states, v_states)], axis=1
        )

    kv_mine = half(core)
    kv_other = lax.ppermute(half(1 - core), "tensor", swap)
    first, second = (jnp.where(core == 0, a, b) for a, b in ((kv_mine, kv_other), (kv_other, kv_mine)))
    kv_chip = jnp.concatenate([first, second], axis=0)
    kv_chip, q_states, out_grad = lax.optimization_barrier((kv_chip, q_states, out_grad))
    def later(x, n):
        return lax.ppermute(x, "tensor", [(t, t + 2 * n) for t in range(size - 2 * n)])

    kv1, kv2 = later(kv_chip, 1), later(kv_chip, 2)
    kvs = [later(jnp.concatenate([kv2, kv1], axis=0), 2), kv2, kv1, kv_chip]

    pieces = []
    for g in range(HEADS):
        head = HEADS * (1 - core) + g
        pieces += [heads_of(q_states, head, wide), heads_of(out_grad, head, wide)]
    pieces.append(jnp.broadcast_to(advantage.astype(bf16)[:, None], (ROWS, HD)))
    rq = lax.ppermute(jnp.concatenate(pieces, axis=1), "tensor", swap)
    lens = lax.optimization_barrier((lengths[0], kv2))[0]

    segment, position, length = window_layout(lens, chip * CHIP)
    frequency = rope_base ** (-jnp.arange(HD // 2, dtype=f32) * 2.0 / HD)
    angles = position.astype(f32)[:, None] * frequency[None, :]
    c, s = jnp.cos(angles), jnp.sin(angles)
    cos = jnp.concatenate([c, c], axis=1)
    sin = jnp.concatenate([-s, s], axis=1)
    lane = jnp.arange(HD, dtype=jnp.int32)[None, :]
    same = segment[:, None] == lane
    kaug = jnp.where(same | (lane >= lengths.shape[1]), 0.0, far).astype(bf16)
    qaug = same[BACK * CHIP :].astype(bf16)
    wt = []
    for who, adv in ((core, advantage), (1 - core, rq[:, 2 * HEADS * wide])):
        resp = lax.dynamic_slice_in_dim(length, BACK * CHIP + who * ROWS, ROWS, 0)
        wt.append(adv.astype(f32) / 32.0 * (group_rows / lengths.shape[1]) / resp.astype(f32))
    wt = jnp.stack(wt, axis=1)

    core_arr = core.astype(jnp.int32)[None]
    qt, gt = queries(core_arr, q_states, out_grad, rq, cos, sin, qaug, wt, q_gain[None])
    outs = attend(core_arr, qt, gt, q_states, rq, kvs, cos, sin, kaug, q_gain[None], k_gain[None])
    dq_mine, dq_far, *parts, dkv, gain_rows = outs

    gains = jnp.sum(gain_rows.reshape(2, 8, HD), axis=1)
    gains = gains.reshape(1, 2 * HD)

    def gathered_sum(x, axis):
        n = lax.axis_size(axis)
        spread = jnp.broadcast_to(x[None], (n, 1, 2 * HD))
        return jnp.sum(lax.all_to_all(spread, axis, 0, 0, tiled=True), axis=0)

    dq_back = lax.ppermute(dq_far, "tensor", swap)

    def earlier(x, n):
        return lax.ppermute(x, "tensor", [(t + 2 * n, t) for t in range(size - 2 * n)])

    back = [earlier(part, n) for n, part in zip(range(BACK, 0, -1), parts)]
    gains, back = lax.optimization_barrier((gathered_sum(gains, "dp"), back))
    gains = gathered_sum(gains, "tensor")
    for part in back:
        dkv = dkv + part.astype(f32)
    dkv = dkv.astype(bf16)
    dkv_mine = lax.dynamic_slice_in_dim(dkv, core * ROWS, ROWS, 0)
    dkv_far = lax.ppermute(lax.dynamic_slice_in_dim(dkv, (1 - core) * ROWS, ROWS, 0), "tensor", swap)

    def placed(mine, other):
        return jnp.where(
            core == 0, jnp.concatenate([mine, other], axis=1), jnp.concatenate([other, mine], axis=1)
        )

    def part_of(x, which):
        return jnp.concatenate([x[:, (2 * g + which) * HD : (2 * g + which + 1) * HD] for g in range(HEADS)], axis=1)

    k_grad = placed(part_of(dkv_mine, 0), part_of(dkv_far, 0))
    v_grad = placed(part_of(dkv_mine, 1), part_of(dkv_far, 1))
    q_grad = placed(dq_mine, dq_back)
    return q_grad, k_grad, v_grad, gains.reshape(2, HD) / group_rows


def solution(mesh):
    return jax.shard_map(
        local,
        mesh=mesh,
        in_specs=(
            P(("dp", "tensor"), None),
            P(("dp", "tensor"), None),
            P(("dp", "tensor"), None),
            P(),
            P(),
            P(("dp", "tensor"), None),
            P("dp", None),
            P(("dp", "tensor")),
        ),
        out_specs=(
            P(("dp", "tensor"), None),
            P(("dp", "tensor"), None),
            P(("dp", "tensor"), None),
            P(),
        ),
        check_vma=False,
    )
```

```python
import math

import jax
import jax.numpy as jnp
from jax import lax
from jax.experimental import pallas as pl
from jax.experimental.pallas import tpu as pltpu
from jax.sharding import PartitionSpec as P

HD = 128
GROUP = 8
ROWS = 128
CHIP = 2 * ROWS
HEADS = 2
BACK = 4
WIN = (BACK + 1) * CHIP
SPAN = BACK * CHIP + ROWS
PART = SPAN // 3
SUB = 64
PAIR = 2 * ROWS

rope_base = 1000000.0
norm_eps = 1e-06
far = -1e30
SCALE = 1.0 / math.sqrt(HD)
SCALE2 = SCALE * math.log2(math.e)
f32 = jnp.float32
bf16 = jnp.bfloat16


def unit_of(raw):
    x = raw.astype(f32)
    inv = lax.rsqrt(jnp.mean(x * x, axis=-1, keepdims=True) + norm_eps)
    return x * inv, inv


def turn(scaled, cos, sin):
    return scaled * cos + pltpu.roll(scaled, HD // 2, 1) * sin


def norm_back(d, unit, inv, gain, cos, sin):
    d_scaled = d * cos - pltpu.roll(d, HD // 2, 1) * sin
    prod = d_scaled * unit
    d_unit = d_scaled * gain
    mean = jnp.mean(prod * gain, axis=-1, keepdims=True)
    part = jnp.sum(prod.reshape(prod.shape[0] // 8, 8, HD), axis=0)
    return (d_unit - unit * mean) * inv, part


def attend_kernel(
    core_ref, qt, gt, q_own, q_far, kv_far, kv2, kv1, kv0, cos, sin, kaug, qgain, kgain,
    dq_own, dq_far, dkv4, dkv3, dkv2, dkv1, dkv0, gains,
    kt, vt, s_buf, dp_buf, p_scr, ds_scr, dk_acc, dv_acc,
):
    core = core_ref[0]
    blocks = (kv_far.at[:CHIP], kv_far.at[CHIP:], kv2, kv1, kv0)
    d_blocks = (dkv4, dkv3, dkv2, dkv1, dkv0)
    kg = kgain[...]
    qg = qgain[...]
    for i, blk in enumerate(blocks):
        rows = slice(i * CHIP, (i + 1) * CHIP)
        unit, _ = unit_of(blk[:, :HD])
        kt[rows, :HD] = turn(unit * kg, cos[rows, :], sin[rows, :]).astype(bf16)
        kt[rows, HD:] = kaug[rows, :]
        vt[rows, :] = blk[:, HD:]
    offs = [pl.multiple_of(b * ROWS, ROWS) for b in (core, 1 - core)]

    dk_acc[...] = jnp.zeros_like(dk_acc)
    dv_acc[...] = jnp.zeros_like(dv_acc)
    tiles = [(j, hp) for j in range(2) for hp in range(GROUP // 2)]
    total = len(tiles)
    chunks = SPAN // PART
    nt = (((1,), (1,)), ((), ()))
    tn = (((0,), (0,)), ((), ()))
    nn = (((1,), (0,)), ((), ()))
    key_row = lax.broadcasted_iota(jnp.int32, (ROWS, PAIR), 0)
    query = lax.broadcasted_iota(jnp.int32, (ROWS, PAIR), 1) % ROWS
    causal = key_row <= query
    gain_rows = [jnp.zeros((8, HD), f32)]
    peaks, sums, dots, shift, delta = {}, {}, {}, {}, {}

    def fold(x, op):
        out = x[:8]
        for r in range(8, x.shape[0], 8):
            out = op(out, x[r : r + 8])
        return out

    def cols_of(n):
        hp = tiles[n][1]
        return slice(hp * PAIR, (hp + 1) * PAIR)

    def keys_of(n, c):
        return pl.ds(pl.multiple_of(offs[tiles[n][0]] + c * PART, ROWS), PART)

    def scores(n, c):
        j = tiles[n][0]
        here = slice(c * PART, (c + 1) * PART)
        s = lax.dot_general(kt[keys_of(n, c), :], qt[0, j, cols_of(n), :], nt, preferred_element_type=f32)
        if c == chunks - 1:
            s = jnp.concatenate([s[: PART - ROWS], jnp.where(causal, s[PART - ROWS :], far)], axis=0)
        s_buf[n % 3, here, :] = s
        top = fold(s, jnp.maximum)
        peaks[n] = jnp.maximum(peaks[n], top) if c else top
        dp_buf[n % 3, here, :] = lax.dot_general(
            vt[keys_of(n, c), :], gt[0, j, cols_of(n), :], nt, preferred_element_type=f32
        )

    def weights(n, c):
        if c == 0:
            shift[n] = jnp.max(peaks[n], axis=0, keepdims=True) * SCALE2
            sums[n] = dots[n] = 0.0
        for r in range(c * PART, (c + 1) * PART, SUB):
            e = jnp.exp2(s_buf[n % 3, r : r + SUB, :] * SCALE2 - shift[n])
            sums[n] = sums[n] + fold(e, jnp.add)
            dots[n] = dots[n] + fold(e * dp_buf[n % 3, r : r + SUB, :], jnp.add)

    def slopes(n, c):
        if c == 0:
            norm = jnp.sum(sums[n], axis=0, keepdims=True)
            delta[n] = jnp.sum(dots[n], axis=0, keepdims=True) / norm
            shift[n] = shift[n] + jnp.log2(norm)
        j = tiles[n][0]
        for r in range(c * PART, (c + 1) * PART, SUB):
            p = jnp.exp2(s_buf[n % 3, r : r + SUB, :] * SCALE2 - shift[n])
            p_scr[j, r : r + SUB, cols_of(n)] = p.astype(bf16)
            ds_scr[j, r : r + SUB, cols_of(n)] = (p * (dp_buf[n % 3, r : r + SUB, :] - delta[n]) * SCALE).astype(bf16)

    def query_grads(n):
        j, hp = tiles[n]
        kw = kt[pl.ds(offs[j], SPAN), :HD]
        dq = lax.dot_general(ds_scr[j, :, cols_of(n)], kw, tn, preferred_element_type=f32)
        c = cos[pl.ds(BACK * CHIP + offs[j], ROWS), :]
        s = sin[pl.ds(BACK * CHIP + offs[j], ROWS), :]
        for u in range(2):
            h = hp * 2 + u
            cols = slice(h * HD, (h + 1) * HD)
            raw = q_own[:, cols] if j == 0 else q_far[:, cols]
            unit, inv = unit_of(raw)
            grad, part = norm_back(dq[u * ROWS : (u + 1) * ROWS, :], unit, inv, qg, c, s)
            gain_rows[0] = gain_rows[0] + part
            if j == 0:
                dq_own[:, cols] = grad.astype(bf16)
            else:
                dq_far[:, cols] = grad.astype(bf16)

    def key_grads(n, c):
        j, hp = tiles[n]
        both = slice((hp - 1) * PAIR, (hp + 1) * PAIR)
        here = slice(c * PART, (c + 1) * PART)
        keys = keys_of(n, c)
        dv_acc[keys, :] += lax.dot_general(p_scr[j, here, both], gt[0, j, both, :], nn, preferred_element_type=f32)
        dk_acc[keys, :] += lax.dot_general(ds_scr[j, here, both], qt[0, j, both, :HD], nn, preferred_element_type=f32)

    for step in range(total + 3):
        for c in range(chunks):
            if step < total:
                scores(step, c)
            if 0 <= step - 1 < total:
                weights(step - 1, c)
            if 0 <= step - 2 < total:
                slopes(step - 2, c)
            n = step - 3
            if 0 <= n < total and n % 2 == 1:
                key_grads(n, c)
        if 0 <= step - 3 < total:
            query_grads(step - 3)

    k_rows = jnp.zeros((8, HD), f32)
    for i, (blk, out) in enumerate(zip(blocks, d_blocks)):
        rows = slice(i * CHIP, (i + 1) * CHIP)
        unit, inv = unit_of(blk[:, :HD])
        grad, part = norm_back(dk_acc[rows, :], unit, inv, kg, cos[rows, :], sin[rows, :])
        k_rows = k_rows + part
        out[:, :HD] = grad.astype(out.dtype)
        out[:, HD:] = dv_acc[rows, :].astype(out.dtype)
    rows = jnp.concatenate([gain_rows[0], k_rows], axis=0)
    begun = pl.program_id(0) > 0
    gains[...] = rows + jnp.where(begun, gains[...], 0.0)


def query_kernel(core_ref, q_own, g_own, rq, cos, sin, qaug, wt, qgain, qt, gt):
    core = core_ref[0]
    gain = qgain[...]
    for j in range(2):
        at = pl.ds(pl.multiple_of((core if j == 0 else 1 - core) * ROWS, ROWS), ROWS)
        c, s, hot = cos[at, :], sin[at, :], qaug[at, :]
        for h in range(GROUP):
            cols = slice(h * HD, (h + 1) * HD)
            rows = slice(h * ROWS, (h + 1) * ROWS)
            unit, _ = unit_of(q_own[:, cols] if j == 0 else rq[:, cols])
            qt[0, j, rows, :HD] = turn(unit * gain, c, s).astype(bf16)
            qt[0, j, rows, HD:] = hot
            grad = g_own[:, cols] if j == 0 else rq[:, GROUP * HD + h * HD : GROUP * HD + (h + 1) * HD]
            gt[0, j, rows, :] = (grad.astype(f32) * wt[:, j : j + 1]).astype(bf16)


def queries(core, q_states, out_grad, rq, cos, sin, qaug, wt, qgain):
    wide = GROUP * HD

    def whole(shape, at=(0, 0)):
        return pl.BlockSpec(shape, lambda g, c: at)

    mine = pl.BlockSpec((ROWS, wide), lambda g, c: (0, 2 * c[0] + g))
    own_rows = whole((CHIP, HD), (BACK, 0))
    out = (HEADS, 2, GROUP * ROWS)
    size = 1
    for n in out:
        size *= n
    return pl.pallas_call(
        query_kernel,
        grid_spec=pltpu.PrefetchScalarGridSpec(
            num_scalar_prefetch=1,
            grid=(HEADS,),
            in_specs=[mine, mine, pl.BlockSpec((ROWS, 2 * wide), lambda g, c: (0, g)), own_rows, own_rows]
            + [whole((CHIP, HD)), whole((ROWS, 2)), whole((1, HD))],
            out_specs=[
                pl.BlockSpec((1, 2, GROUP * ROWS, n), lambda g, c: (g, 0, 0, 0)) for n in (2 * HD, HD)
            ],
        ),
        out_shape=[jax.ShapeDtypeStruct(out + (n,), bf16) for n in (2 * HD, HD)],
        compiler_params=pltpu.CompilerParams(vmem_limit_bytes=38 * 2**20),
        cost_estimate=pl.CostEstimate(flops=40 * size * HD, bytes_accessed=5 * 2**20, transcendentals=size),
        name="queries",
    )(core, q_states, out_grad, rq, cos, sin, qaug, wt, qgain)


def attend(core, qt, gt, q_states, rq, kvs, cos, sin, kaug, qgain, kgain):
    wide = GROUP * HD

    def whole(shape):
        return pl.BlockSpec(shape, lambda g, c: (0,) * len(shape))

    def column(shape):
        return pl.BlockSpec(shape, lambda g, c: (0, g))

    mine = pl.BlockSpec((ROWS, wide), lambda g, c: (0, 2 * c[0] + g))
    sds = jax.ShapeDtypeStruct
    pairs = HEADS * 2 * GROUP * ROWS * SPAN
    return pl.pallas_call(
        attend_kernel,
        grid_spec=pltpu.PrefetchScalarGridSpec(
            num_scalar_prefetch=1,
            grid=(HEADS,),
            in_specs=[
                pl.BlockSpec((1, 2, GROUP * ROWS, n), lambda g, c: (g, 0, 0, 0)) for n in (2 * HD, HD)
            ]
            + [mine, pl.BlockSpec((ROWS, wide), lambda g, c: (0, 2 * g))]
            + [column((2 * CHIP, 2 * HD))] + [column((CHIP, 2 * HD))] * 3
            + [whole((WIN, HD))] * 3
            + [whole((1, HD)), whole((1, HD))],
            out_specs=[column((ROWS, wide))] * 2
            + [column((CHIP, 2 * HD))] * (BACK + 1)
            + [whole((16, HD))],
            scratch_shapes=[
                pltpu.VMEM((WIN, 2 * HD), bf16),
                pltpu.VMEM((WIN, HD), bf16),
                pltpu.VMEM((3, SPAN, PAIR), f32),
                pltpu.VMEM((3, SPAN, PAIR), f32),
                pltpu.VMEM((2, SPAN, GROUP * ROWS), bf16),
                pltpu.VMEM((2, SPAN, GROUP * ROWS), bf16),
                pltpu.VMEM((WIN, HD), f32),
                pltpu.VMEM((WIN, HD), f32),
            ],
        ),
        out_shape=[sds((ROWS, HEADS * wide), bf16)] * 2
        + [sds((CHIP, HEADS * 2 * HD), bf16)] * BACK
        + [sds((CHIP, HEADS * 2 * HD), f32), sds((16, HD), f32)],
        compiler_params=pltpu.CompilerParams(vmem_limit_bytes=38 * 2**20),
        cost_estimate=pl.CostEstimate(flops=pairs * HD * 2 * 5, bytes_accessed=4 * 2**20, transcendentals=pairs),
        name="attend_back",
    )(core, qt, gt, q_states, rq, *kvs, cos, sin, kaug, qgain, kgain)


def window_layout(lens, first):
    ends = jnp.cumsum(lens)
    token = first - BACK * CHIP + jnp.arange(WIN, dtype=jnp.int32)
    ended = ends[None, :] <= token[:, None]
    start = jnp.sum(jnp.where(ended, lens[None, :], 0), axis=1)
    segment = jnp.sum(ended.astype(jnp.int32), axis=1)
    owner = segment[:, None] == jnp.arange(lens.shape[0], dtype=jnp.int32)[None, :]
    length = jnp.sum(jnp.where(owner, lens[None, :], 0), axis=1)
    return jnp.where(token < 0, -1, segment), token - start, length


def local(q_states, k_states, v_states, q_gain, k_gain, out_grad, lengths, advantage):
    size = lax.axis_size("tensor")
    pos = lax.axis_index("tensor")
    core = pos % 2
    chip = pos // 2
    chips = size // 2
    group_rows = size * ROWS
    wide = GROUP * HD

    swap = [(t, t ^ 1) for t in range(size)]

    def heads_of(x, g, width):
        return lax.dynamic_slice_in_dim(x, g * width, width, 1)

    def half(who):
        return jnp.concatenate(
            [heads_of(y, HEADS * who + g, HD) for g in range(HEADS) for y in (k_states, v_states)], axis=1
        )

    kv_mine = half(core)
    kv_other = lax.ppermute(half(1 - core), "tensor", swap)
    first, second = (jnp.where(core == 0, a, b) for a, b in ((kv_mine, kv_other), (kv_other, kv_mine)))
    kv_chip = jnp.concatenate([first, second], axis=0)
    kv_chip, q_states, out_grad = lax.optimization_barrier((kv_chip, q_states, out_grad))
    def later(x, n):
        return lax.ppermute(x, "tensor", [(t, t + 2 * n) for t in range(size - 2 * n)])

    kv1, kv2 = later(kv_chip, 1), later(kv_chip, 2)
    kvs = [later(jnp.concatenate([kv2, kv1], axis=0), 2), kv2, kv1, kv_chip]

    pieces = []
    for g in range(HEADS):
        head = HEADS * (1 - core) + g
        pieces += [heads_of(q_states, head, wide), heads_of(out_grad, head, wide)]
    pieces.append(jnp.broadcast_to(advantage.astype(bf16)[:, None], (ROWS, HD)))
    rq = lax.ppermute(jnp.concatenate(pieces, axis=1), "tensor", swap)
    lens = lax.optimization_barrier((lengths[0], kv2))[0]

    segment, position, length = window_layout(lens, chip * CHIP)
    frequency = rope_base ** (-jnp.arange(HD // 2, dtype=f32) * 2.0 / HD)
    angles = position.astype(f32)[:, None] * frequency[None, :]
    c, s = jnp.cos(angles), jnp.sin(angles)
    cos = jnp.concatenate([c, c], axis=1)
    sin = jnp.concatenate([-s, s], axis=1)
    lane = jnp.arange(HD, dtype=jnp.int32)[None, :]
    same = segment[:, None] == lane
    kaug = jnp.where(same | (lane >= lengths.shape[1]), 0.0, far).astype(bf16)
    qaug = same[BACK * CHIP :].astype(bf16)
    wt = []
    for who, adv in ((core, advantage), (1 - core, rq[:, 2 * HEADS * wide])):
        resp = lax.dynamic_slice_in_dim(length, BACK * CHIP + who * ROWS, ROWS, 0)
        wt.append(adv.astype(f32) / 32.0 * (group_rows / lengths.shape[1]) / resp.astype(f32))
    wt = jnp.stack(wt, axis=1)

    core_arr = core.astype(jnp.int32)[None]
    qt, gt = queries(core_arr, q_states, out_grad, rq, cos, sin, qaug, wt, q_gain[None])
    outs = attend(core_arr, qt, gt, q_states, rq, kvs, cos, sin, kaug, q_gain[None], k_gain[None])
    dq_mine, dq_far, *parts, dkv, gain_rows = outs

    gains = jnp.sum(gain_rows.reshape(2, 8, HD), axis=1)
    gains = gains.reshape(1, 2 * HD)

    def gathered_sum(x, axis):
        n = lax.axis_size(axis)
        spread = jnp.broadcast_to(x[None], (n, 1, 2 * HD))
        return jnp.sum(lax.all_to_all(spread, axis, 0, 0, tiled=True), axis=0)

    dq_back = lax.ppermute(dq_far, "tensor", swap)

    def earlier(x, n):
        return lax.ppermute(x, "tensor", [(t + 2 * n, t) for t in range(size - 2 * n)])

    back = [earlier(part, n) for n, part in zip(range(BACK, 0, -1), parts)]
    for part in back:
        dkv = dkv + part.astype(f32)
    gains, dkv = lax.optimization_barrier((gathered_sum(gains, "dp"), dkv.astype(bf16)))
    gains = gathered_sum(gains, "tensor")
    dkv_mine = lax.dynamic_slice_in_dim(dkv, core * ROWS, ROWS, 0)
    dkv_far = lax.ppermute(lax.dynamic_slice_in_dim(dkv, (1 - core) * ROWS, ROWS, 0), "tensor", swap)

    def placed(mine, other):
        return jnp.where(
            core == 0, jnp.concatenate([mine, other], axis=1), jnp.concatenate([other, mine], axis=1)
        )

    def part_of(x, which):
        return jnp.concatenate([x[:, (2 * g + which) * HD : (2 * g + which + 1) * HD] for g in range(HEADS)], axis=1)

    k_grad = placed(part_of(dkv_mine, 0), part_of(dkv_far, 0))
    v_grad = placed(part_of(dkv_mine, 1), part_of(dkv_far, 1))
    q_grad = placed(dq_mine, dq_back)
    return q_grad, k_grad, v_grad, gains.reshape(2, HD) / group_rows


def solution(mesh):
    return jax.shard_map(
        local,
        mesh=mesh,
        in_specs=(
            P(("dp", "tensor"), None),
            P(("dp", "tensor"), None),
            P(("dp", "tensor"), None),
            P(),
            P(),
            P(("dp", "tensor"), None),
            P("dp", None),
            P(("dp", "tensor")),
        ),
        out_specs=(
            P(("dp", "tensor"), None),
            P(("dp", "tensor"), None),
            P(("dp", "tensor"), None),
            P(),
        ),
        check_vma=False,
    )
```
